32 devices in a mesh: groups: 2 (over y), tensor: 16 (over z, x, core).
Axes of the slice: x: 2, y: 2, z: 4, core: 2. Of those that a mesh axis runs over, the one named last changes fastest.
Arguments:
- activations: bfloat16 [64, 16384], P('groups', 'tensor'), parts along dimension 0
- signs: int32 [16384], P('tensor'), may hold values from -1 to 1, as said below
Outputs:
- hessian: float32 [32768, 16384], P(('groups', 'tensor')), parts along dimension 0
The draws below stay inside these ranges and needn't reach their ends.
There are 2 independent parts, one for each index of `groups`. The reference program is written for one: setup_inputs(seed, part) draws one part's arguments, and reference() takes and returns one part's arrays. A program takes and returns all parts, laid end to end along the dimension named above; an argument that names none is the same for every part. Nothing has to cross between parts.
Inputs may be any that keep to these rules, and one draw needn't show every extreme that they name: `signs`: each entry is -1 or +1.
All inputs are finite; a program needn't handle non-finite values.
Results may differ from the reference program's by a relative error of at most 0.0057.
Values may be sent and summed in bfloat16 or wider, within the bound.
No kernel may reach another device: no remote copies, remote signals or barrier semaphores. Data moves between devices by JAX's collectives and lax.ppermute only.
A program may use at most 384 MiB of HBM per device.

```python
import jax
import jax.numpy as jnp
from jax import lax

D = 16384
INNER_ORDER = 128
OUTER_ORDER = 128
TOKENS = 32


def draw_activations(key, part):
    key = jax.random.fold_in(key, 1)
    first, second, third = jax.random.split(key, 3)
    column_scale = jnp.exp(jax.random.uniform(first, (1, D), jnp.float32, 0.0, 2.3))
    row_scale = jnp.exp(jax.random.uniform(second, (TOKENS, 1), jnp.float32, 0.0, 2.3))
    base = jax.random.normal(third, (TOKENS, D), jnp.float32)
    return (0.1 * base * column_scale * row_scale).astype(jnp.bfloat16)


def draw_signs(key, part):
    key = jax.random.fold_in(key, 2)
    return (2 * jax.random.randint(key, (D,), 0, 2) - 1).astype(jnp.int32)


def setup_inputs(seed: int = 0, part: int = 0) -> dict:
    streams_of = jax.random.split(jax.random.key(seed), 3)
    part_keys = jax.random.split(jax.random.fold_in(streams_of[2], part), 3)
    activations = draw_activations(jax.random.fold_in(jax.random.fold_in(streams_of[2], part), 71), part)
    signs = draw_signs(jax.random.fold_in(streams_of[2], 71), part)
    return {"activations": activations, "signs": signs}


def hadamard_matrix(order):
    first = jnp.arange(order, dtype=jnp.int32)[:, None]
    second = jnp.arange(order, dtype=jnp.int32)[None, :]
    count = jnp.zeros((order, order), jnp.int32)
    for level in range(max(order.bit_length() - 1, 0)):
        count = count + jnp.right_shift(first, level) % 2 * (jnp.right_shift(second, level) % 2)
    return jnp.where(count % 2 == 0, 1.0, -1.0).astype(jnp.float32)

def reference(activations, signs):
    token_batch = activations.shape[0]
    sign_flipped = activations.astype(jnp.float32) * signs.astype(jnp.float32)[None, :]
    inner_block = jnp.einsum('lgu,uq->lgq', sign_flipped.reshape(token_batch, OUTER_ORDER, INNER_ORDER), hadamard_matrix(INNER_ORDER)) / jnp.sqrt(jnp.float32(INNER_ORDER))
    inner_block = inner_block.astype(jnp.bfloat16).astype(jnp.float32)
    outer = jnp.einsum('tab,ae->teb', inner_block, hadamard_matrix(OUTER_ORDER)) / jnp.sqrt(jnp.float32(OUTER_ORDER))
    rotated_input = outer.reshape(token_batch, D).astype(jnp.bfloat16)
    gram = lax.dot_general(rotated_input, rotated_input, (((0,), (0,)), ((), ())), preferred_element_type=jnp.float32)
    return gram / jnp.float32(token_batch)
```

```python
import functools

import jax
import jax.numpy as jnp
from jax import lax
from jax.experimental import pallas as pl
from jax.experimental.pallas import tpu as pltpu
from jax.sharding import PartitionSpec as P

LANES = 128
CHUNK = 512
BUFFERS = 4


def butterfly(terms):
    step = 1
    while step < len(terms):
        out = list(terms)
        for low in range(len(terms)):
            if not low & step:
                out[low] = terms[low] + terms[low | step]
                out[low | step] = terms[low] - terms[low | step]
        terms = out
        step *= 2
    return terms


def odd_bits(value, order):
    shift = 1
    while shift < order.bit_length():
        shift *= 2
    while shift:
        value = value ^ (value >> shift)
        shift //= 2
    return value & 1


def hessian_kernel(ranks, mine_ref, other_ref, out_ref, wide, rotated, own_rows, tiles, sems):
    me = lax.axis_index("tensor")
    half, tokens, columns = mine_ref.shape
    local = columns // LANES
    width = ranks * columns

    row = lax.broadcasted_iota(jnp.int32, (LANES, LANES), 0)
    col = lax.broadcasted_iota(jnp.int32, (LANES, LANES), 1)
    inner = ((1 - 2 * odd_bits(row & col, LANES)).astype(jnp.float32) * (1.0 / LANES)).astype(jnp.bfloat16)
    for offset, ref in ((0, mine_ref), (1, other_ref)):

        @pl.loop(0, half)
        def _(k):
            block = ref[k]
            stacked = jnp.concatenate([block[:, j * LANES : (j + 1) * LANES] for j in range(local)], axis=0)
            spread = jnp.dot(stacked, inner, preferred_element_type=jnp.float32)
            terms = butterfly([spread[j * tokens : (j + 1) * tokens] for j in range(local)])
            for j in range(local):
                wide[2 * k + offset, j] = terms[j]

    signs = [(1 - 2 * odd_bits(me & m, ranks)).astype(jnp.float32) for m in range(ranks)]

    @pl.loop(0, local)
    def _(j):
        @pl.loop(0, tokens // 16)
        def _(t):
            rows = pl.ds(pl.multiple_of(t * 16, 16), 16)
            terms = butterfly([wide[k, j, rows, :] for k in range(ranks)])
            for m in range(ranks):
                at = pl.ds(pl.multiple_of((m * local + j) * LANES, LANES), LANES)
                rotated[rows, at] = (terms[m] * signs[m]).astype(jnp.bfloat16)

    own_rows[...] = rotated[:, pl.ds(pl.multiple_of(me * columns, LANES), columns)].T

    def copy(step, slot):
        at = pl.ds(pl.multiple_of(step * CHUNK, CHUNK), CHUNK)
        return pltpu.make_async_copy(tiles.at[slot], out_ref.at[:, at], sems.at[slot])

    @pl.loop(0, width // CHUNK // BUFFERS)
    def _(turn):
        for slot in range(BUFFERS):
            step = turn * BUFFERS + slot

            @pl.when(turn > 0)
            def _():
                copy(step - BUFFERS, slot).wait()

            at = pl.ds(pl.multiple_of(step * CHUNK, CHUNK), CHUNK)
            tiles[slot] = jnp.dot(own_rows[...], rotated[:, at], preferred_element_type=jnp.float32) * (1.0 / tokens)
            copy(step, slot).start()

    for slot in range(BUFFERS):
        copy(width // CHUNK - BUFFERS + slot, slot).wait()


def hessian_rows(ranks, mine, other):
    half, tokens, columns = mine.shape
    width = ranks * columns
    return pl.pallas_call(
        functools.partial(hessian_kernel, ranks),
        in_specs=[pl.BlockSpec(memory_space=pltpu.VMEM)] * 2,
        out_specs=pl.BlockSpec(memory_space=pl.ANY),
        out_shape=jax.ShapeDtypeStruct((columns, width), jnp.float32),
        scratch_shapes=[
            pltpu.VMEM((ranks, columns // LANES, tokens, LANES), jnp.float32),
            pltpu.VMEM((tokens, width), jnp.bfloat16),
            pltpu.VMEM((columns, tokens), jnp.bfloat16),
            pltpu.VMEM((BUFFERS, columns, CHUNK), jnp.float32),
            pltpu.SemaphoreType.DMA((BUFFERS,)),
        ],
        compiler_params=pltpu.CompilerParams(vmem_limit_bytes=40 * 2**20),
        cost_estimate=pl.CostEstimate(
            flops=2 * tokens * columns * width, bytes_accessed=4 * columns * width, transcendentals=0
        ),
    )(mine, other)


def per_device(ranks, activations, signs):
    flipped = activations * signs.astype(jnp.bfloat16)[None, :]

    def from_partner(x, k):
        return lax.ppermute(x, "tensor", [(i, i ^ k) for i in range(ranks)])

    far = range(4, ranks, 4)
    blocks = {0: flipped}
    for k in far:
        blocks[k] = from_partner(flipped, k)
    blocks[2] = from_partner(flipped, 2)
    crossed = from_partner(jnp.stack([blocks[k] for k in far]), 2)
    for i, k in enumerate(far):
        blocks[k + 2] = crossed[i]
    mine = jnp.stack([blocks[k] for k in range(0, ranks, 2)])
    return hessian_rows(ranks, mine, from_partner(mine, 1))


def solution(mesh):
    return jax.shard_map(
        functools.partial(per_device, mesh.shape["tensor"]),
        mesh=mesh,
        in_specs=(P("groups", "tensor"), P("tensor")),
        out_specs=P(("groups", "tensor"), None),
        check_vma=False,
    )
```

```python
import functools

import jax
import jax.numpy as jnp
from jax import lax
from jax.experimental import pallas as pl
from jax.experimental.pallas import tpu as pltpu
from jax.sharding import PartitionSpec as P

LANES = 128
CHUNK = 512
BUFFERS = 4
UNROLL = 8


def butterfly(terms):
    step = 1
    while step < len(terms):
        out = list(terms)
        for low in range(len(terms)):
            if not low & step:
                out[low] = terms[low] + terms[low | step]
                out[low | step] = terms[low] - terms[low | step]
        terms = out
        step *= 2
    return terms


def odd_bits(value, order):
    shift = 1
    while shift < order.bit_length():
        shift *= 2
    while shift:
        value = value ^ (value >> shift)
        shift //= 2
    return value & 1


def in_turns(steps):
    unroll = min(UNROLL, steps)

    def run(body):
        @pl.loop(0, steps // unroll)
        def _(turn):
            for i in range(unroll):
                body(turn * unroll + i)

    return run


def hessian_kernel(ranks, mine_ref, other_ref, out_ref, wide, rotated, own_rows, tiles, sems):
    me = lax.axis_index("tensor")
    half, tokens, columns = mine_ref.shape
    local = columns // LANES
    width = ranks * columns

    row = lax.broadcasted_iota(jnp.int32, (LANES, LANES), 0)
    col = lax.broadcasted_iota(jnp.int32, (LANES, LANES), 1)
    inner = ((1 - 2 * odd_bits(row & col, LANES)).astype(jnp.float32) * (1.0 / LANES)).astype(jnp.bfloat16)
    for offset, ref in ((0, mine_ref), (1, other_ref)):

        @in_turns(half)
        def _(k):
            block = ref[k]
            stacked = jnp.concatenate([block[:, j * LANES : (j + 1) * LANES] for j in range(local)], axis=0)
            spread = jnp.dot(stacked, inner, preferred_element_type=jnp.float32)
            terms = butterfly([spread[j * tokens : (j + 1) * tokens] for j in range(local)])
            for j in range(local):
                wide[2 * k + offset, j] = terms[j]

    signs = [(1 - 2 * odd_bits(me & m, ranks)).astype(jnp.float32) for m in range(ranks)]

    pieces = tokens // 16

    @in_turns(local * pieces)
    def _(piece):
        j = piece // pieces
        rows = pl.ds(pl.multiple_of(piece % pieces * 16, 16), 16)
        terms = butterfly([wide[k, j, rows, :] for k in range(ranks)])
        for m in range(ranks):
            at = pl.ds(pl.multiple_of((m * local + j) * LANES, LANES), LANES)
            rotated[rows, at] = (terms[m] * signs[m]).astype(jnp.bfloat16)

    own_rows[...] = rotated[:, pl.ds(pl.multiple_of(me * columns, LANES), columns)].T

    def copy(step, slot):
        at = pl.ds(pl.multiple_of(step * CHUNK, CHUNK), CHUNK)
        return pltpu.make_async_copy(tiles.at[slot], out_ref.at[:, at], sems.at[slot])

    @pl.loop(0, width // CHUNK // BUFFERS)
    def _(turn):
        for slot in range(BUFFERS):
            step = turn * BUFFERS + slot

            @pl.when(turn > 0)
            def _():
                copy(step - BUFFERS, slot).wait()

            at = pl.ds(pl.multiple_of(step * CHUNK, CHUNK), CHUNK)
            tiles[slot] = jnp.dot(own_rows[...], rotated[:, at], preferred_element_type=jnp.float32) * (1.0 / tokens)
            copy(step, slot).start()

    for slot in range(BUFFERS):
        copy(width // CHUNK - BUFFERS + slot, slot).wait()


def hessian_rows(ranks, mine, other):
    half, tokens, columns = mine.shape
    width = ranks * columns
    return pl.pallas_call(
        functools.partial(hessian_kernel, ranks),
        in_specs=[pl.BlockSpec(memory_space=pltpu.VMEM)] * 2,
        out_specs=pl.BlockSpec(memory_space=pl.ANY),
        out_shape=jax.ShapeDtypeStruct((columns, width), jnp.float32),
        scratch_shapes=[
            pltpu.VMEM((ranks, columns // LANES, tokens, LANES), jnp.float32),
            pltpu.VMEM((tokens, width), jnp.bfloat16),
            pltpu.VMEM((columns, tokens), jnp.bfloat16),
            pltpu.VMEM((BUFFERS, columns, CHUNK), jnp.float32),
            pltpu.SemaphoreType.DMA((BUFFERS,)),
        ],
        compiler_params=pltpu.CompilerParams(vmem_limit_bytes=40 * 2**20),
        cost_estimate=pl.CostEstimate(
            flops=2 * tokens * columns * width, bytes_accessed=4 * columns * width, transcendentals=0
        ),
    )(mine, other)


def per_device(ranks, activations, signs):
    flipped = activations * signs.astype(jnp.bfloat16)[None, :]

    def from_partner(x, k):
        return lax.ppermute(x, "tensor", [(i, i ^ k) for i in range(ranks)])

    far = range(4, ranks, 4)
    blocks = {0: flipped}
    for k in far:
        blocks[k] = from_partner(flipped, k)
    blocks[2] = from_partner(flipped, 2)
    crossed = from_partner(jnp.stack([blocks[k] for k in far]), 2)
    for i, k in enumerate(far):
        blocks[k + 2] = crossed[i]
    mine = jnp.stack([blocks[k] for k in range(0, ranks, 2)])
    return hessian_rows(ranks, mine, from_partner(mine, 1))


def solution(mesh):
    return jax.shard_map(
        functools.partial(per_device, mesh.shape["tensor"]),
        mesh=mesh,
        in_specs=(P("groups", "tensor"), P("tensor")),
        out_specs=P(("groups", "tensor"), None),
        check_vma=False,
    )
```

```python
import functools

import jax
import jax.numpy as jnp
from jax import lax
from jax.experimental import pallas as pl
from jax.experimental.pallas import tpu as pltpu
from jax.sharding import PartitionSpec as P

LANES = 128
CHUNK = 512
BUFFERS = 4
UNROLL = 8


def butterfly(terms):
    step = 1
    while step < len(terms):
        out = list(terms)
        for low in range(len(terms)):
            if not low & step:
                out[low] = terms[low] + terms[low | step]
                out[low | step] = terms[low] - terms[low | step]
        terms = out
        step *= 2
    return terms


def odd_bits(value, order):
    shift = 1
    while shift < order.bit_length():
        shift *= 2
    while shift:
        value = value ^ (value >> shift)
        shift //= 2
    return value & 1


def in_turns(steps):
    unroll = min(UNROLL, steps)

    def run(body):
        @pl.loop(0, steps // unroll)
        def _(turn):
            for i in range(unroll):
                body(turn * unroll + i)

    return run


def hessian_kernel(ranks, mine_ref, other_ref, out_ref, wide, rotated, own_rows, tiles, sems):
    me = lax.axis_index("tensor")
    half, tokens, columns = mine_ref.shape
    local = columns // LANES
    width = ranks * columns

    row = lax.broadcasted_iota(jnp.int32, (LANES, LANES), 0)
    col = lax.broadcasted_iota(jnp.int32, (LANES, LANES), 1)
    inner = ((1 - 2 * odd_bits(row & col, LANES)).astype(jnp.float32) * (1.0 / LANES)).astype(jnp.bfloat16)
    for offset, ref in ((0, mine_ref), (1, other_ref)):

        @in_turns(half)
        def _(k):
            block = ref[k]
            stacked = jnp.concatenate([block[:, j * LANES : (j + 1) * LANES] for j in range(local)], axis=0)
            spread = jnp.dot(stacked, inner, preferred_element_type=jnp.float32)
            terms = butterfly([spread[j * tokens : (j + 1) * tokens] for j in range(local)])
            for j in range(local):
                wide[2 * k + offset, j] = terms[j]

    signs = [(1 - 2 * odd_bits(me & m, ranks)).astype(jnp.float32) for m in range(ranks)]

    pieces = tokens // 16

    @in_turns(local * pieces)
    def _(piece):
        j = piece // pieces
        rows = pl.ds(pl.multiple_of(piece % pieces * 16, 16), 16)
        terms = butterfly([wide[k, j, rows, :] for k in range(ranks)])
        for m in range(ranks):
            at = pl.ds(pl.multiple_of((m * local + j) * LANES, LANES), LANES)
            rotated[rows, at] = (terms[m] * signs[m]).astype(jnp.bfloat16)

    own_rows[...] = rotated[:, pl.ds(pl.multiple_of(me * columns, LANES), columns)].T

    def copy(step, slot):
        at = pl.ds(pl.multiple_of(step * CHUNK, CHUNK), CHUNK)
        return pltpu.make_async_copy(tiles.at[slot], out_ref.at[:, at], sems.at[slot])

    @pl.loop(0, width // CHUNK // BUFFERS)
    def _(turn):
        for slot in range(BUFFERS):
            step = turn * BUFFERS + slot

            @pl.when(turn > 0)
            def _():
                copy(step - BUFFERS, slot).wait()

            at = pl.ds(pl.multiple_of(step * CHUNK, CHUNK), CHUNK)
            tiles[slot] = jnp.dot(own_rows[...], rotated[:, at], preferred_element_type=jnp.float32) * (1.0 / tokens)
            copy(step, slot).start()

    for slot in range(BUFFERS):
        copy(width // CHUNK - BUFFERS + slot, slot).wait()


def hessian_rows(ranks, mine, other):
    half, tokens, columns = mine.shape
    width = ranks * columns
    return pl.pallas_call(
        functools.partial(hessian_kernel, ranks),
        in_specs=[pl.BlockSpec(memory_space=pltpu.VMEM)] * 2,
        out_specs=pl.BlockSpec(memory_space=pl.ANY),
        out_shape=jax.ShapeDtypeStruct((columns, width), jnp.float32),
        scratch_shapes=[
            pltpu.VMEM((ranks, columns // LANES, tokens, LANES), jnp.float32),
            pltpu.VMEM((tokens, width), jnp.bfloat16),
            pltpu.VMEM((columns, tokens), jnp.bfloat16),
            pltpu.VMEM((BUFFERS, columns, CHUNK), jnp.float32),
            pltpu.SemaphoreType.DMA((BUFFERS,)),
        ],
        compiler_params=pltpu.CompilerParams(vmem_limit_bytes=40 * 2**20),
        cost_estimate=pl.CostEstimate(
            flops=2 * tokens * columns * width, bytes_accessed=4 * columns * width, transcendentals=0
        ),
    )(mine, other)


def per_device(ranks, activations, signs):
    flipped = activations * signs.astype(jnp.bfloat16)[None, :]

    def from_partner(x, k):
        return lax.ppermute(x, "tensor", [(i, i ^ k) for i in range(ranks)])

    def cross(ks):
        crossed = from_partner(jnp.stack([blocks[k] for k in ks]), 2)
        for i, k in enumerate(ks):
            blocks[k + 2] = crossed[i]

    first = ranks // 2
    rest = [k for k in range(ranks - 4, 0, -4) if k != first]
    blocks = {0: flipped}
    for k in [first] + rest:
        blocks[k] = from_partner(flipped, k)
    cross([0, first])
    cross(rest)
    mine = jnp.stack([blocks[k] for k in range(0, ranks, 2)])
    return hessian_rows(ranks, mine, from_partner(mine, 1))


def solution(mesh):
    return jax.shard_map(
        functools.partial(per_device, mesh.shape["tensor"]),
        mesh=mesh,
        in_specs=(P("groups", "tensor"), P("tensor")),
        out_specs=P(("groups", "tensor"), None),
        check_vma=False,
    )
```

```python
import functools

import jax
import jax.numpy as jnp
from jax import lax
from jax.experimental import pallas as pl
from jax.experimental.pallas import tpu as pltpu
from jax.sharding import PartitionSpec as P

LANES = 128
CHUNK = 512
BUFFERS = 4
UNROLL = 8


def butterfly(terms):
    step = 1
    while step < len(terms):
        out = list(terms)
        for low in range(len(terms)):
            if not low & step:
                out[low] = terms[low] + terms[low | step]
                out[low | step] = terms[low] - terms[low | step]
        terms = out
        step *= 2
    return terms


def odd_bits(value, order):
    shift = 1
    while shift < order.bit_length():
        shift *= 2
    while shift:
        value = value ^ (value >> shift)
        shift //= 2
    return value & 1


def in_turns(steps):
    def run(body):
        if steps <= UNROLL:
            for i in range(steps):
                body(i)
            return

        @pl.loop(0, steps // UNROLL)
        def _(turn):
            for i in range(UNROLL):
                body(turn * UNROLL + i)

    return run


def rotate_half(blocks_ref, store):
    half, tokens, columns = blocks_ref.shape
    row = lax.broadcasted_iota(jnp.int32, (LANES, LANES), 0)
    col = lax.broadcasted_iota(jnp.int32, (LANES, LANES), 1)
    inner = ((1 - 2 * odd_bits(row & col, LANES)).astype(jnp.float32) * (1.0 / LANES)).astype(jnp.bfloat16)
    size = min(tokens, max(16, 256 // half))
    pieces = tokens // size

    @in_turns(columns // LANES * pieces)
    def _(piece):
        j = piece // pieces
        rows = pl.ds(piece % pieces * size, size)
        lanes = pl.ds(j * LANES, LANES)
        if not isinstance(piece, int):
            rows = pl.ds(pl.multiple_of(piece % pieces * size, 16), size)
            lanes = pl.ds(pl.multiple_of(j * LANES, LANES), LANES)
        stacked = jnp.concatenate([blocks_ref[k, rows, lanes] for k in range(half)], axis=0)
        spread = jnp.dot(stacked, inner, preferred_element_type=jnp.float32)
        store(j, rows, butterfly([spread[k * size : (k + 1) * size] for k in range(half)]))


def half_kernel(mine_ref, out_ref):
    def store(j, rows, terms):
        for m, term in enumerate(terms):
            out_ref[m, j, rows, :] = term

    rotate_half(mine_ref, store)


def hessian_kernel(ranks, half_ref, other_ref, out_ref, wide, rotated, own_rows, tiles, sems):
    me = lax.axis_index("tensor")
    half, tokens, columns = other_ref.shape
    local = columns // LANES
    width = ranks * columns
    turn_width = BUFFERS * CHUNK

    def store(j, rows, terms):
        for m, term in enumerate(terms):
            mine = half_ref[m, j, rows, :]
            wide[2 * m, j, rows, :] = mine + term
            wide[2 * m + 1, j, rows, :] = mine - term

    rotate_half(other_ref, store)

    def finish(m, start):
        sign = (1 - 2 * odd_bits(me & m, ranks)).astype(jnp.float32)
        for e, term in enumerate(butterfly([wide[m, j] for j in range(local)])):
            rotated[:, start + e * LANES : start + (e + 1) * LANES] = (term * sign).astype(jnp.bfloat16)

    finish(me, 0)
    own_rows[...] = rotated[:, :columns].T

    def copy(step, slot):
        at = pl.ds(pl.multiple_of(step * CHUNK, CHUNK), CHUNK)
        return pltpu.make_async_copy(tiles.at[slot], out_ref.at[:, at], sems.at[slot])

    @pl.loop(0, width // turn_width)
    def _(turn):
        for i in range(turn_width // columns):
            finish(turn * (turn_width // columns) + i, i * columns)
        for slot in range(BUFFERS):
            step = turn * BUFFERS + slot

            @pl.when(turn > 0)
            def _():
                copy(step - BUFFERS, slot).wait()

            rows = rotated[:, slot * CHUNK : (slot + 1) * CHUNK]
            tiles[slot] = jnp.dot(own_rows[...], rows, preferred_element_type=jnp.float32) * (1.0 / tokens)
            copy(step, slot).start()

    for slot in range(BUFFERS):
        copy(width // CHUNK - BUFFERS + slot, slot).wait()


def rotate_mine(mine):
    half, tokens, columns = mine.shape
    return pl.pallas_call(
        half_kernel,
        in_specs=[pl.BlockSpec(memory_space=pltpu.VMEM)],
        out_specs=pl.BlockSpec(memory_space=pltpu.VMEM),
        out_shape=jax.ShapeDtypeStruct((half, columns // LANES, tokens, LANES), jnp.float32),
        compiler_params=pltpu.CompilerParams(vmem_limit_bytes=16 * 2**20),
        cost_estimate=pl.CostEstimate(
            flops=2 * half * tokens * columns * LANES, bytes_accessed=6 * half * tokens * columns, transcendentals=0
        ),
    )(mine)


def hessian_rows(ranks, mine, other):
    half, tokens, columns = other.shape
    width = ranks * columns
    return pl.pallas_call(
        functools.partial(hessian_kernel, ranks),
        in_specs=[pl.BlockSpec(memory_space=pltpu.VMEM)] * 2,
        out_specs=pl.BlockSpec(memory_space=pl.ANY),
        out_shape=jax.ShapeDtypeStruct((columns, width), jnp.float32),
        scratch_shapes=[
            pltpu.VMEM((ranks, columns // LANES, tokens, LANES), jnp.float32),
            pltpu.VMEM((tokens, BUFFERS * CHUNK), jnp.bfloat16),
            pltpu.VMEM((columns, tokens), jnp.bfloat16),
            pltpu.VMEM((BUFFERS, columns, CHUNK), jnp.float32),
            pltpu.SemaphoreType.DMA((BUFFERS,)),
        ],
        compiler_params=pltpu.CompilerParams(vmem_limit_bytes=40 * 2**20),
        cost_estimate=pl.CostEstimate(
            flops=2 * tokens * columns * width, bytes_accessed=4 * columns * width, transcendentals=0
        ),
    )(mine, other)


def per_device(ranks, activations, signs):
    sign = jnp.where(activations == 0, 1, lax.broadcast_in_dim(signs, activations.shape, (1,)))
    flipped = activations * sign.astype(jnp.bfloat16)

    def from_partner(x, k):
        return lax.ppermute(x, "tensor", [(i, i ^ k) for i in range(ranks)])

    def cross(ks):
        crossed = from_partner(jnp.stack([blocks[k] for k in ks]), 2)
        for i, k in enumerate(ks):
            blocks[k + 2] = crossed[i]

    first = ranks // 2
    rest = [k for k in range(ranks - 4, 0, -4) if k != first]
    blocks = {0: flipped}
    for k in [first] + rest:
        blocks[k] = from_partner(flipped, k)
    cross([0, first])
    cross(rest)
    mine = jnp.stack([blocks[k] for k in range(0, ranks, 2)])
    return hessian_rows(ranks, rotate_mine(mine), from_partner(mine, 1))


def solution(mesh):
    return jax.shard_map(
        functools.partial(per_device, mesh.shape["tensor"]),
        mesh=mesh,
        in_specs=(P("groups", "tensor"), P("tensor")),
        out_specs=P(("groups", "tensor"), None),
        check_vma=False,
    )
```

```python
import functools

import jax
import jax.numpy as jnp
from jax import lax
from jax.experimental import pallas as pl
from jax.experimental.pallas import tpu as pltpu
from jax.sharding import PartitionSpec as P

LANES = 128
CHUNK = 512
BUFFERS = 4
UNROLL = 8


def butterfly(terms):
    step = 1
    while step < len(terms):
        out = list(terms)
        for low in range(len(terms)):
            if not low & step:
                first, second = terms[low], terms[low | step]
                if first is None and second is not None:
                    out[low], out[low | step] = second, -second
                elif second is None:
                    out[low], out[low | step] = first, first
                else:
                    out[low], out[low | step] = first + second, first - second
        terms = out
        step *= 2
    return terms


def odd_bits(value, order):
    shift = 1
    while shift < order.bit_length():
        shift *= 2
    while shift:
        value = value ^ (value >> shift)
        shift //= 2
    return value & 1


def in_turns(steps):
    def run(body):
        if steps <= UNROLL:
            for i in range(steps):
                body(i)
            return

        @pl.loop(0, steps // UNROLL)
        def _(turn):
            for i in range(UNROLL):
                body(turn * UNROLL + i)

    return run


def rotate_half(half, sources, store):
    _, tokens, columns = sources[0][0].shape
    row = lax.broadcasted_iota(jnp.int32, (LANES, LANES), 0)
    col = lax.broadcasted_iota(jnp.int32, (LANES, LANES), 1)
    inner = ((1 - 2 * odd_bits(row & col, LANES)).astype(jnp.float32) * (1.0 / LANES)).astype(jnp.bfloat16)
    size = min(tokens, max(16, 256 // half))
    pieces = tokens // size

    @in_turns(columns // LANES * pieces)
    def _(piece):
        j = piece // pieces
        rows = pl.ds(piece % pieces * size, size)
        lanes = pl.ds(j * LANES, LANES)
        if not isinstance(piece, int):
            rows = pl.ds(pl.multiple_of(piece % pieces * size, 16), size)
            lanes = pl.ds(pl.multiple_of(j * LANES, LANES), LANES)
        stacked = jnp.concatenate([ref[i, rows, lanes] for ref, at in sources for i in range(len(at))], axis=0)
        spread = jnp.dot(stacked, inner, preferred_element_type=jnp.float32)
        terms = [None] * half
        for i, k in enumerate(k for _, at in sources for k in at):
            terms[k] = spread[i * size : (i + 1) * size]
        store(j, rows, butterfly(terms))


def mine_kernel(early_at, late_at, early_ref, late_ref, out_ref):
    def store(j, rows, terms):
        for m, term in enumerate(terms):
            out_ref[m, j, rows, :] = term

    rotate_half(len(early_at) + len(late_at), [(early_ref, early_at), (late_ref, late_at)], store)


def early_kernel(early_at, half_ref, other_ref, out_ref):
    def store(j, rows, terms):
        for m, term in enumerate(terms):
            mine = half_ref[m, j, rows, :]
            out_ref[2 * m, j, rows, :] = mine + term
            out_ref[2 * m + 1, j, rows, :] = mine - term

    rotate_half(half_ref.shape[0], [(other_ref, early_at)], store)


def hessian_kernel(ranks, late_at, wide_ref, late_ref, out_ref, late, rotated, own_rows, tiles, sems):
    me = lax.axis_index("tensor")
    _, tokens, columns = late_ref.shape
    local = columns // LANES
    width = ranks * columns
    turn_width = BUFFERS * CHUNK

    def store(j, rows, terms):
        for m, term in enumerate(terms):
            late[m, j, rows, :] = term

    rotate_half(ranks // 2, [(late_ref, late_at)], store)

    def finish(m, start):
        sign = (1 - 2 * odd_bits(me & m, ranks)).astype(jnp.float32)
        side = (1 - 2 * (m & 1)).astype(jnp.float32)
        terms = [wide_ref[m, j] + side * late[m // 2, j] for j in range(local)]
        for e, term in enumerate(butterfly(terms)):
            rotated[:, start + e * LANES : start + (e + 1) * LANES] = (term * sign).astype(jnp.bfloat16)

    finish(me, 0)
    own_rows[...] = rotated[:, :columns].T

    def copy(step, slot):
        at = pl.ds(pl.multiple_of(step * CHUNK, CHUNK), CHUNK)
        return pltpu.make_async_copy(tiles.at[slot], out_ref.at[:, at], sems.at[slot])

    @pl.loop(0, width // turn_width)
    def _(turn):
        for i in range(turn_width // columns):
            finish(turn * (turn_width // columns) + i, i * columns)
        for slot in range(BUFFERS):
            step = turn * BUFFERS + slot

            @pl.when(turn > 0)
            def _():
                copy(step - BUFFERS, slot).wait()

            rows = rotated[:, slot * CHUNK : (slot + 1) * CHUNK]
            tiles[slot] = jnp.dot(own_rows[...], rows, preferred_element_type=jnp.float32) * (1.0 / tokens)
            copy(step, slot).start()

    for slot in range(BUFFERS):
        copy(width // CHUNK - BUFFERS + slot, slot).wait()


def stack_kernel(*refs):
    for i, ref in enumerate(refs[:-1]):
        refs[-1][i] = ref[...]


def stack(blocks, flops):
    shape = (len(blocks),) + blocks[0].shape
    return pl.pallas_call(
        stack_kernel,
        in_specs=[pl.BlockSpec(memory_space=pltpu.VMEM)] * len(blocks),
        out_specs=pl.BlockSpec(memory_space=pltpu.VMEM),
        out_shape=jax.ShapeDtypeStruct(shape, blocks[0].dtype),
        compiler_params=pltpu.CompilerParams(vmem_limit_bytes=16 * 2**20),
        cost_estimate=pl.CostEstimate(flops=flops, bytes_accessed=flops // 300, transcendentals=0),
    )(*blocks)


def in_vmem(kernel, shape, *operands):
    return pl.pallas_call(
        kernel,
        in_specs=[pl.BlockSpec(memory_space=pltpu.VMEM)] * len(operands),
        out_specs=pl.BlockSpec(memory_space=pltpu.VMEM),
        out_shape=jax.ShapeDtypeStruct(shape, jnp.float32),
        compiler_params=pltpu.CompilerParams(vmem_limit_bytes=40 * 2**20),
        cost_estimate=pl.CostEstimate(flops=10**6, bytes_accessed=10**4, transcendentals=0),
    )(*operands)


def hessian_rows(ranks, late_at, wide, late):
    _, tokens, columns = late.shape
    width = ranks * columns
    return pl.pallas_call(
        functools.partial(hessian_kernel, ranks, late_at),
        in_specs=[pl.BlockSpec(memory_space=pltpu.VMEM)] * 2,
        out_specs=pl.BlockSpec(memory_space=pl.ANY),
        out_shape=jax.ShapeDtypeStruct((columns, width), jnp.float32),
        scratch_shapes=[
            pltpu.VMEM((ranks // 2, columns // LANES, tokens, LANES), jnp.float32),
            pltpu.VMEM((tokens, BUFFERS * CHUNK), jnp.bfloat16),
            pltpu.VMEM((columns, tokens), jnp.bfloat16),
            pltpu.VMEM((BUFFERS, columns, CHUNK), jnp.float32),
            pltpu.SemaphoreType.DMA((BUFFERS,)),
        ],
        compiler_params=pltpu.CompilerParams(vmem_limit_bytes=40 * 2**20),
        cost_estimate=pl.CostEstimate(
            flops=2 * tokens * columns * width, bytes_accessed=4 * columns * width, transcendentals=0
        ),
    )(wide, late)


def per_device(ranks, activations, signs):
    sign = jnp.where(activations == 0, 1, lax.broadcast_in_dim(signs, activations.shape, (1,)))
    flipped = activations * sign.astype(jnp.bfloat16)

    def from_partner(x, k):
        return lax.ppermute(x, "tensor", [(i, i ^ k) for i in range(ranks)])

    def cross(ks, flops):
        crossed = from_partner(stack([blocks[k] for k in ks], flops), 2)
        for i, k in enumerate(ks):
            blocks[k + 2] = crossed[i]

    first = ranks // 2
    rest = [k for k in range(4, ranks, 4) if k != first]
    blocks = {0: flipped}
    for k in [first] + rest + [2]:
        blocks[k] = from_partner(flipped, k)
    blocks[rest[-1]] = stack([blocks[rest[-1]]], 3 * 10**9)[0]
    cross([first], 0)
    cross(rest, 3 * 10**10)
    late_ks = [k + 2 for k in rest]
    early_ks = [k for k in range(0, ranks, 2) if k not in late_ks]
    early_at = [k // 2 for k in early_ks]
    late_at = [k // 2 for k in late_ks]
    early = jnp.stack([blocks[k] for k in early_ks])
    late = stack([blocks[k] for k in late_ks], 3 * 10**10)
    shape = (activations.shape[1] // LANES, activations.shape[0], LANES)
    half = in_vmem(functools.partial(mine_kernel, early_at, late_at), (ranks // 2,) + shape, early, late)
    wide = in_vmem(functools.partial(early_kernel, early_at), (ranks,) + shape, half, from_partner(early, 1))
    return hessian_rows(ranks, late_at, wide, from_partner(late, 1))


def solution(mesh):
    return jax.shard_map(
        functools.partial(per_device, mesh.shape["tensor"]),
        mesh=mesh,
        in_specs=(P("groups", "tensor"), P("tensor")),
        out_specs=P(("groups", "tensor"), None),
        check_vma=False,
    )
```

```python
import functools

import jax
import jax.numpy as jnp
from jax import lax
from jax.experimental import pallas as pl
from jax.experimental.pallas import tpu as pltpu
from jax.sharding import PartitionSpec as P

LANES = 128
CHUNK = 512
BUFFERS = 4
UNROLL = 8


def butterfly(terms):
    step = 1
    while step < len(terms):
        out = list(terms)
        for low in range(len(terms)):
            if not low & step:
                first, second = terms[low], terms[low | step]
                if first is None and second is not None:
                    out[low], out[low | step] = second, -second
                elif second is None:
                    out[low], out[low | step] = first, first
                else:
                    out[low], out[low | step] = first + second, first - second
        terms = out
        step *= 2
    return terms


def odd_bits(value, order):
    shift = 1
    while shift < order.bit_length():
        shift *= 2
    while shift:
        value = value ^ (value >> shift)
        shift //= 2
    return value & 1


def in_turns(steps):
    def run(body):
        if steps <= UNROLL:
            for i in range(steps):
                body(i)
            return

        @pl.loop(0, steps // UNROLL)
        def _(turn):
            for i in range(UNROLL):
                body(turn * UNROLL + i)

    return run


def rotate_half(half, sources, store):
    _, tokens, columns = sources[0][0].shape
    row = lax.broadcasted_iota(jnp.int32, (LANES, LANES), 0)
    col = lax.broadcasted_iota(jnp.int32, (LANES, LANES), 1)
    inner = ((1 - 2 * odd_bits(row & col, LANES)).astype(jnp.float32) * (1.0 / LANES)).astype(jnp.bfloat16)
    size = min(tokens, max(16, 256 // half))
    pieces = tokens // size

    @in_turns(columns // LANES * pieces)
    def _(piece):
        j = piece // pieces
        rows = pl.ds(piece % pieces * size, size)
        lanes = pl.ds(j * LANES, LANES)
        if not isinstance(piece, int):
            rows = pl.ds(pl.multiple_of(piece % pieces * size, 16), size)
            lanes = pl.ds(pl.multiple_of(j * LANES, LANES), LANES)
        stacked = jnp.concatenate([ref[i, rows, lanes] for ref, at in sources for i in range(len(at))], axis=0)
        spread = jnp.dot(stacked, inner, preferred_element_type=jnp.float32)
        terms = [None] * half
        for i, k in enumerate(k for _, at in sources for k in at):
            terms[k] = spread[i * size : (i + 1) * size]
        store(j, rows, butterfly(terms))


def mine_kernel(early_at, late_at, early_ref, late_ref, out_ref):
    def store(j, rows, terms):
        for m, term in enumerate(terms):
            out_ref[m, j, rows, :] = term

    rotate_half(len(early_at) + len(late_at), [(early_ref, early_at), (late_ref, late_at)], store)


def early_kernel(early_at, half_ref, other_ref, out_ref):
    def store(j, rows, terms):
        for m, term in enumerate(terms):
            mine = half_ref[m, j, rows, :]
            out_ref[2 * m, j, rows, :] = mine + term
            out_ref[2 * m + 1, j, rows, :] = mine - term

    rotate_half(half_ref.shape[0], [(other_ref, early_at)], store)


def hessian_kernel(ranks, late_at, wide_ref, late_ref, out_ref, late, rotated, own_rows, tiles, sems):
    me = lax.axis_index("tensor")
    _, tokens, columns = late_ref.shape
    local = columns // LANES
    width = ranks * columns
    turn_width = BUFFERS * CHUNK

    def store(j, rows, terms):
        for m, term in enumerate(terms):
            late[m, j, rows, :] = term

    rotate_half(ranks // 2, [(late_ref, late_at)], store)

    def finish(m, start):
        sign = (1 - 2 * odd_bits(me & m, ranks)).astype(jnp.float32)
        side = (1 - 2 * (m & 1)).astype(jnp.float32)
        terms = [wide_ref[m, j] + side * late[m // 2, j] for j in range(local)]
        for e, term in enumerate(butterfly(terms)):
            rotated[:, start + e * LANES : start + (e + 1) * LANES] = (term * sign).astype(jnp.bfloat16)

    finish(me, 0)
    own_rows[...] = rotated[:, :columns].T

    def copy(step, slot):
        at = pl.ds(pl.multiple_of(step * CHUNK, CHUNK), CHUNK)
        return pltpu.make_async_copy(tiles.at[slot], out_ref.at[:, at], sems.at[slot])

    @pl.loop(0, width // turn_width)
    def _(turn):
        for slot in range(BUFFERS):
            step = turn * BUFFERS + slot
            for i in range(turn_width // columns):
                if i * columns // CHUNK == slot:
                    finish(turn * (turn_width // columns) + i, i * columns)

            @pl.when(turn > 0)
            def _():
                copy(step - BUFFERS, slot).wait()

            rows = rotated[:, slot * CHUNK : (slot + 1) * CHUNK]
            tiles[slot] = jnp.dot(own_rows[...], rows, preferred_element_type=jnp.float32) * (1.0 / tokens)
            copy(step, slot).start()

    for slot in range(BUFFERS):
        copy(width // CHUNK - BUFFERS + slot, slot).wait()


def stack_kernel(*refs):
    for i, ref in enumerate(refs[:-1]):
        refs[-1][i] = ref[...]


def stack(blocks, flops):
    shape = (len(blocks),) + blocks[0].shape
    return pl.pallas_call(
        stack_kernel,
        in_specs=[pl.BlockSpec(memory_space=pltpu.VMEM)] * len(blocks),
        out_specs=pl.BlockSpec(memory_space=pltpu.VMEM),
        out_shape=jax.ShapeDtypeStruct(shape, blocks[0].dtype),
        compiler_params=pltpu.CompilerParams(vmem_limit_bytes=16 * 2**20),
        cost_estimate=pl.CostEstimate(flops=flops, bytes_accessed=flops // 300, transcendentals=0),
    )(*blocks)


def in_vmem(kernel, shape, *operands):
    return pl.pallas_call(
        kernel,
        in_specs=[pl.BlockSpec(memory_space=pltpu.VMEM)] * len(operands),
        out_specs=pl.BlockSpec(memory_space=pltpu.VMEM),
        out_shape=jax.ShapeDtypeStruct(shape, jnp.float32),
        compiler_params=pltpu.CompilerParams(vmem_limit_bytes=40 * 2**20),
        cost_estimate=pl.CostEstimate(flops=10**6, bytes_accessed=10**4, transcendentals=0),
    )(*operands)


def hessian_rows(ranks, late_at, wide, late):
    _, tokens, columns = late.shape
    width = ranks * columns
    return pl.pallas_call(
        functools.partial(hessian_kernel, ranks, late_at),
        in_specs=[pl.BlockSpec(memory_space=pltpu.VMEM)] * 2,
        out_specs=pl.BlockSpec(memory_space=pl.ANY),
        out_shape=jax.ShapeDtypeStruct((columns, width), jnp.float32),
        scratch_shapes=[
            pltpu.VMEM((ranks // 2, columns // LANES, tokens, LANES), jnp.float32),
            pltpu.VMEM((tokens, BUFFERS * CHUNK), jnp.bfloat16),
            pltpu.VMEM((columns, tokens), jnp.bfloat16),
            pltpu.VMEM((BUFFERS, columns, CHUNK), jnp.float32),
            pltpu.SemaphoreType.DMA((BUFFERS,)),
        ],
        compiler_params=pltpu.CompilerParams(vmem_limit_bytes=40 * 2**20),
        cost_estimate=pl.CostEstimate(
            flops=2 * tokens * columns * width, bytes_accessed=4 * columns * width, transcendentals=0
        ),
    )(wide, late)


def per_device(ranks, activations, signs):
    sign = jnp.where(activations == 0, 1, lax.broadcast_in_dim(signs, activations.shape, (1,)))
    flipped = activations * sign.astype(jnp.bfloat16)

    def from_partner(x, k):
        return lax.ppermute(x, "tensor", [(i, i ^ k) for i in range(ranks)])

    def cross(ks, flops):
        crossed = from_partner(stack([blocks[k] for k in ks], flops), 2)
        for i, k in enumerate(ks):
            blocks[k + 2] = crossed[i]

    first = ranks // 2
    rest = [k for k in range(4, ranks, 4) if k != first]
    blocks = {0: flipped}
    for k in [first] + rest + [2]:
        blocks[k] = from_partner(flipped, k)
    blocks[rest[-1]] = stack([blocks[rest[-1]]], 3 * 10**9)[0]
    cross([first], 0)
    cross(rest, 3 * 10**10)
    late_ks = [k + 2 for k in rest]
    early_ks = [k for k in range(0, ranks, 2) if k not in late_ks]
    early_at = [k // 2 for k in early_ks]
    late_at = [k // 2 for k in late_ks]
    early = jnp.stack([blocks[k] for k in early_ks])
    late = stack([blocks[k] for k in late_ks], 3 * 10**10)
    shape = (activations.shape[1] // LANES, activations.shape[0], LANES)
    half = in_vmem(functools.partial(mine_kernel, early_at, late_at), (ranks // 2,) + shape, early, late)
    wide = in_vmem(functools.partial(early_kernel, early_at), (ranks,) + shape, half, from_partner(early, 1))
    return hessian_rows(ranks, late_at, wide, from_partner(late, 1))


def solution(mesh):
    return jax.shard_map(
        functools.partial(per_device, mesh.shape["tensor"]),
        mesh=mesh,
        in_specs=(P("groups", "tensor"), P("tensor")),
        out_specs=P(("groups", "tensor"), None),
        check_vma=False,
    )
```
